128 devices in a mesh: group: 2 (over core), dev: 64 (over z, x, y).
Axes of the slice: x: 4, y: 4, z: 4, core: 2. Of those that a mesh axis runs over, the one named last changes fastest.
Arguments:
- tokens: bfloat16 [2048, 7168], P('dev', 'group'), may hold values from -6 to 6
- routes: int32 [2048, 8], P('dev'), may hold values from 0 to 63, all different within a row; in each aligned block of 32 rows (0 to 31, 32 to 63, ...) at most 10 rows name the same one
- route_weights: float32 [2048, 8], P('dev'), may hold values from 0.05 to 0.6
- placement: int32 [64], replicated, may hold values from 0 to 63, each once
- w_gate: bfloat16 [64, 7168, 1024], P('dev', None, 'group'), may hold values from -0.0625 to 0.0625
- w_up: bfloat16 [64, 7168, 1024], P('dev', None, 'group'), may hold values from -0.0625 to 0.0625
- w_down: bfloat16 [64, 1024, 7168], P('dev', 'group'), may hold values from -0.1875 to 0.1875
Outputs:
- expert_mix: bfloat16 [2048, 7168], P('dev', 'group')
The draws below stay inside these ranges and needn't reach their ends.
Inputs may be any that keep to these rules, and one draw needn't show every extreme that they name: `routes`: in the rows of one device (aligned blocks of 32 rows) no expert is named by more than 10 rows; a row names 8 different experts. `placement`: a permutation: every slot holds one expert.
All inputs are finite; a program needn't handle non-finite values.
Results may differ from the reference program's by a relative error of at most 0.025.
Values may be sent and summed in bfloat16 or wider, within the bound.
A program may use at most 192 MiB of HBM per device.

```python
import math
import jax
import jax.numpy as jnp
import numpy as np
from jax import lax

D = 7168
HID = 1024
TOP = 8
SEQ_DEV = 32
SEQS = 2048
EXPERTS = 64
MOST = 10
N_GROUP = 2
N_DEV = 64


def block_levels(rng, shape, pieces, least, top_value):
    level = 1.0
    for axis_at, parts in pieces:
        heights = jax.random.uniform(jax.random.fold_in(jax.random.fold_in(rng, 6), axis_at), (parts,), jnp.float32, least / len(pieces), top_value / len(pieces))
        level = level * jnp.repeat(jnp.exp(heights), shape[axis_at] // parts).reshape((-1,) + (1,) * (len(shape) - 1 - axis_at))
    return level


def routed_block(rng, own, number, rows, amount, top, reach, lean):
    sequence = jax.random.permutation(rng, amount)
    heavy_load, ordinary = load_shares(amount, rows * top, reach, lean, True), load_shares(amount, rows * top, reach, lean, False)
    places = jnp.arange(amount)

    def named(sizes, rotation):
        used = int((sizes > 0).sum())
        fixed = max(1, used // 4)
        shifted = fixed + (places - fixed + rotation * (used - fixed)) % max(1, amount - fixed)
        return jnp.zeros((amount,), jnp.int32).at[sequence[jnp.where(places < fixed, places, shifted)]].set(jnp.asarray(sizes, jnp.int32))

    sizes = jnp.where(number % 4 == 0, named(heavy_load, number // 4), named(ordinary, number - number // 4 - 1))
    mixed = jax.random.permutation(jax.random.fold_in(own, 3), amount)
    giver, receiver = mixed[0:amount // 2 * 2:2], mixed[1:amount // 2 * 2:2]
    margin = jnp.minimum(sizes[giver] - 1, reach - sizes[receiver]) // 2
    margin = jnp.where((giver == sequence[0]) | (receiver == sequence[0]) | (sizes[receiver] == 0), 0, jnp.maximum(margin, 0))
    shifted = jax.random.randint(jax.random.fold_in(own, 4), (amount // 2,), 0, 1 << 20) % (margin + 1)
    sizes = sizes.at[giver].add(-shifted).at[receiver].add(shifted)
    items = jnp.searchsorted(jnp.cumsum(sizes), jnp.arange(rows * top), side="right").astype(jnp.int32)
    listing = items.reshape(top, rows).T
    listing = listing[jax.random.permutation(jax.random.fold_in(own, 1), rows)]
    rotation = jax.random.randint(jax.random.fold_in(own, 2), (rows, 1), 0, top)
    return jnp.take_along_axis(listing, (jnp.arange(top)[None, :] + rotation) % top, axis=1)


def load_shares(number_of, total, reach, skew, full):
    loads = [(1 << 20) // math.isqrt(grade ** skew) + 1 for grade in range(1, number_of + 1)]
    largest = reach if full else min(reach, max(-(-total // number_of), total * loads[0] // sum(loads)))
    least = 1 if total - largest >= number_of - 1 else 0
    holding, rest = [largest] + [least] * (number_of - 1), total - largest - least * (number_of - 1)
    while rest > 0:
        movable = [i for i in range(1, number_of) if holding[i] < largest] or [i for i in range(1, number_of) if holding[i] < reach]
        pool, left = sum([loads[i] for i in movable]), rest
        for i in movable:
            addition = min(reach - holding[i], max(1, left * loads[i] // pool), rest)
            holding[i] = holding[i] + addition
            rest = rest - addition
    return np.array(holding)


def noise(stream_key, dims, deviation, most, cuts=(), kind=jnp.bfloat16):
    drawn = deviation * jax.random.normal(stream_key, dims, jnp.float32)
    if cuts:
        drawn = drawn * block_levels(stream_key, dims, cuts, -0.22, 0.18)
    return jnp.clip(drawn, -most, most).astype(kind)


def setup_inputs(seed: int = 0) -> dict:
    key_list = jax.random.split(jax.random.key(seed), 8)
    tokens = noise(key_list[0], (SEQS, D), 1.0, 6.0, ((0, 64), (1, 2)))
    routes_keys = jax.random.split(jax.random.fold_in(key_list[1], 1), SEQS // SEQ_DEV)
    routes_turns = jax.random.permutation(jax.random.fold_in(key_list[1], 3), SEQS // SEQ_DEV)
    routes = jax.vmap(lambda own, number: routed_block(jax.random.fold_in(key_list[1], 2), own, number, SEQ_DEV, EXPERTS, TOP, MOST, 2))(routes_keys, routes_turns).reshape((SEQS, TOP))
    route_weights = jnp.clip(0.05 + 0.55 * jax.random.uniform(key_list[2], (SEQS, TOP), jnp.float32) ** block_levels(key_list[2], (SEQS, TOP), ((0, 64),), -0.2, 0.2), 0.05, 0.6)
    placement = jax.random.permutation(key_list[3], EXPERTS).astype(jnp.int32)
    w_gate = noise(key_list[4], (EXPERTS, D, HID), D ** -0.5, 0.0625, ((0, 64), (2, 2)))
    w_up = noise(key_list[5], (EXPERTS, D, HID), D ** -0.5, 0.0625, ((0, 64), (2, 2)))
    w_down = noise(key_list[6], (EXPERTS, HID, D), HID ** -0.5, 0.1875, ((0, 64), (1, 2)))
    return {"tokens": tokens, "routes": routes, "route_weights": route_weights, "placement": placement, "w_gate": w_gate, "w_up": w_up, "w_down": w_down}


def reference(tokens, routes, route_weights, placement, w_gate, w_up, w_down):
    per_block = SEQ_DEV * TOP
    flat_routes = routes.reshape(N_DEV, per_block)
    onehot = (flat_routes[:, :, None] == jnp.arange(EXPERTS, dtype=jnp.int32)[None, None, :]).astype(jnp.int32)
    position = jnp.sum(jnp.cumsum(onehot, axis=1) * onehot, axis=2) - 1
    destination = placement[flat_routes].astype(jnp.int32)
    source = jnp.broadcast_to(jnp.arange(N_DEV, dtype=jnp.int32)[:, None], (N_DEV, per_block))
    owner = source * SEQ_DEV + jnp.arange(per_block, dtype=jnp.int32)[None, :] // TOP
    slot_index = (source * MOST + position).astype(jnp.int32)
    table = jnp.full((EXPERTS, N_DEV * MOST), SEQS, dtype=jnp.int32)
    table = table.at[destination, slot_index].set(owner.astype(jnp.int32))
    padded = jnp.concatenate([tokens, jnp.zeros((1, D), dtype=tokens.dtype)], axis=0)
    half_width = HID // N_GROUP

    def expert_apply(operands):
        indices, gate_w, up_w, down_w = operands
        token_rows = padded[indices]
        gate = jnp.dot(token_rows, gate_w, preferred_element_type=jnp.float32)
        upper = jnp.dot(token_rows, up_w, preferred_element_type=jnp.float32)
        hidden = (jax.nn.silu(gate) * upper).astype(jnp.bfloat16)
        total = jnp.zeros((token_rows.shape[0], D), dtype=jnp.float32)
        for piece in range(N_GROUP):
            lower = piece * half_width
            section = jnp.dot(hidden[:, lower:lower + half_width], down_w[lower:lower + half_width], preferred_element_type=jnp.float32)
            total = total + lax.optimization_barrier(section.astype(jnp.bfloat16)).astype(jnp.float32)
        return total

    outputs = lax.map(expert_apply, (table, w_gate, w_up, w_down))
    picked = outputs[destination, slot_index].reshape(SEQS, TOP, D)
    expert_mix = jnp.sum(picked * route_weights[:, :, None], axis=1).astype(jnp.bfloat16)
    return expert_mix
```

```python
import jax
import jax.numpy as jnp
import numpy as np
from jax import lax
from jax.experimental import pallas as pl
from jax.experimental.pallas import tpu as pltpu
from jax.sharding import PartitionSpec as P

MESH = pl.DeviceIdType.MESH
BF = jnp.bfloat16
F32 = jnp.float32
CW = 512
MAIN, REST = 8, 2
A_AG, B_AG, C_OUT, C_BACK, B_RS, A_RS = range(6)


def rest_matrices():
    mats = np.zeros((6, 128, 128), np.float32)
    for rho in range(3):
        for q in np.ndindex(4, 4, 4):
            for j in range(REST):

                def row(turn):
                    a, b, c = q[turn], q[(turn + 2) % 3], q[(turn + 1) % 3]
                    return ((b // 2) * 4 + c) * 16 + ((b % 2) * 4 + a) * 2 + j

                mats[rho, row(0), row(rho)] = 1
        mats[3 + rho] = mats[rho].T
    return mats


def main_row(q, rho):
    a, b, c = q[rho], q[(rho + 2) % 3], q[(rho + 1) % 3]
    return ((b // 2) * 4 + c) * 80 + ((b % 2) * 4 + a) * MAIN


def dot(x, y):
    return jnp.dot(x, y, preferred_element_type=F32)


def kernel(
    tok, info, perm, wg_hbm, wu_hbm, wd_hbm, out,
    WG, WU, WD, B, SB, X, XP, acc, HR, RB, RSB, RA, QB, IB, SEL, WT,
    ss, rs, iss, irs, ess, ers, hss, hrs, wsem, dss, drs,
):
    g = lax.axis_index("group")
    dev = lax.axis_index("dev")
    n = B.shape[0]
    half = n * CW

    def stride(ax):
        return lax.div(32 - 33 * ax + 9 * ax * ax, 2)

    def coord(ax):
        return lax.rem(lax.div(dev, stride(ax)), 4)

    def peer(ax, k):
        at = coord(ax)
        return dev + (lax.rem(at + k, 4) - at) * stride(ax)

    def axes(slot, core):
        rho = lax.rem(slot + core, 3)
        return rho, lax.rem(rho + 2, 3), lax.rem(rho + 1, 3)

    def remote(src, dst, s, r, ax, k):
        return pltpu.make_async_remote_copy(
            src, dst, s, r, device_id={"dev": peer(ax, k)}, device_id_type=MESH
        )

    def across(src, dst, s, r):
        return pltpu.make_async_remote_copy(
            src, dst, s, r, device_id={"group": 1 - g}, device_id_type=MESH
        )

    def block(i, size):
        return pl.ds(pl.multiple_of(i * size, size), size)

    def a_ag(i, k):
        a, b, c = axes(lax.rem(i, 3), g)
        here = B.at[i, block(coord(b) * 4 + coord(a), 32)]
        return remote(tok.at[:, block(i, CW)], here, ss.at[A_AG, i, k - 1], rs.at[A_AG, i, k - 1], a, k)

    def b_ag(i, k):
        a, b, c = axes(lax.rem(i, 3), g)
        here = B.at[i, block(coord(b), 128)]
        return remote(here, here, ss.at[B_AG, i, k - 1], rs.at[B_AG, i, k - 1], b, k)

    def c_out(i, k):
        a, b, c = axes(lax.rem(i, 3), g)
        to = lax.rem(coord(c) + k, 4)
        return remote(SB.at[i, :, to], X.at[i, :, coord(c)], ss.at[C_OUT, i, k - 1], rs.at[C_OUT, i, k - 1], c, k)

    def c_back(i, k):
        a, b, c = axes(lax.rem(i, 3), g)
        to = lax.rem(coord(c) + k, 4)
        return remote(SB.at[i, :, to], RB.at[i, :, coord(c)], ss.at[C_BACK, i, k - 1], rs.at[C_BACK, i, k - 1], c, k)

    def b_rs(i, k):
        a, b, c = axes(lax.rem(i, 3), g)
        to = lax.rem(coord(b) + k, 4)
        return remote(B.at[i, block(to, 128)], RSB.at[i, k - 1], ss.at[B_RS, i, k - 1], rs.at[B_RS, i, k - 1], b, k)

    def a_rs(i, k):
        a, b, c = axes(lax.rem(i, 3), g)
        to = lax.rem(coord(a) + k, 4)
        return remote(QB.at[i, block(to, 32)], RA.at[i, k - 1], ss.at[A_RS, i, k - 1], rs.at[A_RS, i, k - 1], a, k)

    def info_a(r, k):
        a, b, c = axes(r, g)
        return remote(info, IB.at[r, coord(b), coord(a)], iss.at[0, r, k - 1], irs.at[0, r, k - 1], a, k)

    def info_b(r, k):
        a, b, c = axes(r, g)
        here = IB.at[r, coord(b)]
        return remote(here, here, iss.at[1, r, k - 1], irs.at[1, r, k - 1], b, k)

    def rows_across(i):
        return across(X.at[i], XP.at[i], ess.at[i], ers.at[i])

    def hidden_across(rho):
        return across(HR.at[rho, g], HR.at[rho, g], hss.at[rho], hrs.at[rho])

    def every(fn):
        def step(i, carry):
            fn(i)
            return carry

        lax.fori_loop(0, n, step, 0)

    bar = pltpu.get_barrier_semaphore()
    for ax in range(3):
        for k in (1, 2, 3):
            pl.semaphore_signal(bar, inc=1, device_id={"dev": peer(ax, k)}, device_id_type=MESH)
    pl.semaphore_signal(bar, inc=1, device_id={"group": 1 - g}, device_id_type=MESH)
    pl.semaphore_wait(bar, 10)

    for r in range(3):
        a, b, c = axes(r, g)
        for k in (1, 2, 3):
            info_a(r, k).start()
        IB[r, coord(b), coord(a)] = info[...]

    @every
    def _(i):
        a, b, c = axes(lax.rem(i, 3), g)
        for k in (1, 2, 3):
            a_ag(i, k).start()
        B[i, block(coord(b) * 4 + coord(a), 32), :] = tok[:, block(i, CW)]

    wg_copy = pltpu.make_async_copy(wg_hbm.at[0], WG, wsem.at[0])
    wu_copy = pltpu.make_async_copy(wu_hbm.at[0], WU, wsem.at[1])
    hid = WG.shape[1]
    wd_copy = pltpu.make_async_copy(wd_hbm.at[0, :, block(g, half)], WD.at[block(g, hid)], wsem.at[2])
    wd_across = across(wd_hbm.at[0, :, block(1 - g, half)], WD.at[block(g, hid)], dss, drs)
    wg_copy.start()
    wu_copy.start()
    wd_copy.start()
    wd_across.start()

    for r in range(3):
        for k in (1, 2, 3):
            info_a(r, k).wait_recv()
        for k in (1, 2, 3):
            info_b(r, k).start()

    @every
    def _(i):
        for k in (1, 2, 3):
            a_ag(i, k).wait_recv()
        for k in (1, 2, 3):
            b_ag(i, k).start()

    acc[...] = jnp.zeros_like(acc)

    lane = lax.broadcasted_iota(jnp.int32, (8, 128), 1)
    seg_mask = [(lane >= 32 * a) & (lane < 32 * a + 32) for a in range(4)]
    lane1 = lax.broadcasted_iota(jnp.int32, (16, 128), 1)
    seg16 = sum(jnp.where(lane1 >= 32 * a, 1, 0) for a in (1, 2, 3))
    row1 = lax.broadcasted_iota(jnp.int32, (16, 128), 0)
    odd_b = jnp.where(((row1 >= 4) & (row1 < 8)) | (row1 >= 12), 1, 0)
    src8 = (odd_b * 4 + seg16).astype(F32)
    ti = lax.broadcasted_iota(jnp.int32, (128, 128), 0)
    tj = lax.broadcasted_iota(jnp.int32, (128, 128), 1)
    start_j = sum(jnp.where(tj >= 32 * a, 32, 0) for a in (1, 2, 3))
    before = jnp.where((ti < tj) & (ti >= start_j), 1.0, 0.0).astype(BF)
    iota_q = lax.broadcasted_iota(jnp.int32, (80, 128), 0).astype(F32)
    iota_k = lax.broadcasted_iota(jnp.int32, (128, 320), 1).astype(F32)

    for r in range(3):
        a_ax, b_ax, c_ax = axes(r, g)
        for k in (1, 2, 3):
            info_b(r, k).wait_recv()
        hits, weights = [], []
        for b in range(4):
            dest = sum(jnp.where(seg_mask[a], IB[r, b, a, 0:8, :], 0.0) for a in range(4))
            wts = sum(jnp.where(seg_mask[a], IB[r, b, a, 8:16, :], 0.0) for a in range(4))
            for d in range(4):
                target = (dev + (d - coord(c_ax)) * stride(c_ax)).astype(F32)
                hit = dest == target
                hits.append(jnp.sum(jnp.where(hit, 1.0, 0.0), axis=0, keepdims=True))
                weights.append(jnp.sum(jnp.where(hit, wts, 0.0), axis=0, keepdims=True))
        hits = jnp.concatenate(hits, axis=0)
        weights = jnp.concatenate(weights, axis=0)
        rank = dot(hits.astype(BF), before)
        place = jnp.where(rank < MAIN, src8 * MAIN + rank, 64 + src8 * REST + (rank - MAIN))
        place = jnp.where(hits > 0, place, -1000.0)
        fill = jnp.zeros((112, 128), F32)
        place_t = jnp.transpose(jnp.concatenate([place, fill], axis=0))
        weights_t = jnp.transpose(jnp.concatenate([weights, fill], axis=0))
        for b in range(4):
            total = jnp.zeros((128, 320), F32)
            for d in range(4):
                at = b * 4 + d
                SEL[r, b // 2, d * 80 : d * 80 + 80, (b % 2) * 128 : (b % 2) * 128 + 128] = jnp.where(
                    iota_q == place[at : at + 1, :], 1.0, 0.0
                ).astype(BF)
                total = total + jnp.where(
                    iota_k == place_t[:, at : at + 1] + 80.0 * d, weights_t[:, at : at + 1], 0.0
                )
            high = total.astype(BF)
            low = (total - high.astype(F32)).astype(BF)
            WT[0, r, b // 2, (b % 2) * 128 : (b % 2) * 128 + 128, :] = high
            WT[1, r, b // 2, (b % 2) * 128 : (b % 2) * 128 + 128, :] = low

    @every
    def _(i):
        r = lax.rem(i, 3)
        a, b, c = axes(r, g)
        for k in (1, 2, 3):
            b_ag(i, k).wait_recv()
        for h in range(2):
            picked = dot(SEL[r, h], B[i, h * 256 : h * 256 + 256, :]).astype(BF)
            SB[i, h] = picked.reshape(4, 80, CW)
        for k in (1, 2, 3):
            c_out(i, k).start()
        X[i, :, coord(c)] = SB[i, :, coord(c)]

    wg_copy.wait()
    wu_copy.wait()

    def multiply(rows_ref, i, core):
        rho, _, _ = axes(lax.rem(i, 3), core)
        rows = rows_ref[i].reshape(640, CW)
        depth = pl.ds(pl.multiple_of(core * half + i * CW, CW), CW)
        for w, weight in enumerate((WG, WU)):
            for part in range(2):
                cols = slice(part * 256, part * 256 + 256)
                acc[w, rho, :, cols] += dot(rows, weight[depth, cols])

    @every
    def _(i):
        rho, _, _ = axes(lax.rem(i, 3), g)
        for k in (1, 2, 3):
            c_out(i, k).wait_recv()
        rest = jnp.concatenate([X[i, h, c, 64:80, :] for h in range(2) for c in range(4)], axis=0)
        rest = dot(perm[rho], rest).astype(BF)
        for h in range(2):
            for c in range(4):
                at = (h * 4 + c) * 16
                X[i, h, c, 64:80, :] = rest[at : at + 16, :]
        rows_across(i).start()
        multiply(X, i, g)
        rows_across(i).wait_recv()
        multiply(XP, i, 1 - g)

    def swiglu(gate, up):
        return gate / (1.0 + jnp.exp(-gate)) * up

    for q in np.ndindex(4, 4, 4):
        rows = [slice(main_row(q, rho), main_row(q, rho) + MAIN) for rho in range(3)]
        gate = acc[0, 0, rows[0], :] + acc[0, 1, rows[1], :] + acc[0, 2, rows[2], :]
        up = acc[1, 0, rows[0], :] + acc[1, 1, rows[1], :] + acc[1, 2, rows[2], :]
        acc[0, 0, rows[0], :] = swiglu(gate, up)
    for m in range(8):
        rows = slice(m * 80 + 64, m * 80 + 80)
        gate = acc[0, 0, rows, :] + acc[0, 1, rows, :] + acc[0, 2, rows, :]
        up = acc[1, 0, rows, :] + acc[1, 1, rows, :] + acc[1, 2, rows, :]
        acc[0, 0, rows, :] = swiglu(gate, up)

    rest = jnp.concatenate([acc[0, 0, m * 80 + 64 : m * 80 + 80, :] for m in range(8)], axis=0).astype(BF)
    for rho in range(3):
        for q in np.ndindex(4, 4, 4):
            if q[rho] % 2:
                continue
            two = list(q)
            two[rho] += 1
            here = main_row(q, rho)
            one, other = main_row(q, 0), main_row(two, 0)
            HR[rho, g, here : here + 16, :] = jnp.concatenate(
                [acc[0, 0, one : one + MAIN, :], acc[0, 0, other : other + MAIN, :]], axis=0
            ).astype(BF)
        turned = dot(perm[3 + rho], rest).astype(BF)
        for m in range(8):
            HR[rho, g, m * 80 + 64 : m * 80 + 80, :] = turned[m * 16 : m * 16 + 16, :]
        hidden_across(rho).start()

    wd_copy.wait()
    wd_across.wait()
    for rho in range(3):
        hidden_across(rho).wait_recv()

    @every
    def _(i):
        rho, _, c = axes(lax.rem(i, 3), g)
        for k in (1, 2, 3):
            c_out(i, k).wait_send()
        for part in range(2):
            cols = pl.ds(pl.multiple_of(i * CW + part * 256, 256), 256)
            made = dot(HR[rho, 0], WD[0:hid, cols]) + dot(HR[rho, 1], WD[hid : 2 * hid, cols])
            SB[i, :, :, :, part * 256 : part * 256 + 256] = made.astype(BF).reshape(2, 4, 80, 256)
        for k in (1, 2, 3):
            c_back(i, k).start()
        RB[i, :, coord(c)] = SB[i, :, coord(c)]

    @every
    def _(i):
        r = lax.rem(i, 3)
        for k in (1, 2, 3):
            c_back(i, k).wait_recv()
            b_ag(i, k).wait_send()
        for h in range(2):
            rows = RB[i, h].reshape(320, CW)
            B[i, h * 256 : h * 256 + 256, :] = (dot(WT[0, r, h], rows) + dot(WT[1, r, h], rows)).astype(BF)
        for k in (1, 2, 3):
            b_rs(i, k).start()

    @every
    def _(i):
        a, b, c = axes(lax.rem(i, 3), g)
        for k in (1, 2, 3):
            b_rs(i, k).wait_recv()
        total = B[i, block(coord(b), 128), :].astype(F32)
        for k in range(3):
            total = total + RSB[i, k].astype(F32)
        QB[i] = total.astype(BF)
        for k in (1, 2, 3):
            a_rs(i, k).start()

    @every
    def _(i):
        a, b, c = axes(lax.rem(i, 3), g)
        for k in (1, 2, 3):
            a_rs(i, k).wait_recv()
        total = QB[i, block(coord(a), 32), :].astype(F32)
        for k in range(3):
            total = total + RA[i, k].astype(F32)
        out[:, block(i, CW)] = total.astype(BF)

    @every
    def _(i):
        for k in (1, 2, 3):
            a_ag(i, k).wait_send()
            c_back(i, k).wait_send()
            b_rs(i, k).wait_send()
            a_rs(i, k).wait_send()
        rows_across(i).wait_send()

    for r in range(3):
        for k in (1, 2, 3):
            info_a(r, k).wait_send()
            info_b(r, k).wait_send()
        hidden_across(r).wait_send()


def body(tokens, routes, route_weights, placement, w_gate, w_up, w_down):
    local_tokens, half = tokens.shape
    experts = placement.shape[0]
    n = half // CW
    hid = w_gate.shape[2]
    onehot = routes.T[:, :, None] == jnp.arange(experts, dtype=jnp.int32)[None, None, :]
    destination = jnp.sum(jnp.where(onehot, placement[None, None, :], 0), axis=2).astype(F32)
    info = jnp.tile(jnp.concatenate([destination, route_weights.T], axis=0), (1, 4))
    perm = jnp.asarray(rest_matrices(), BF)
    vmem = pl.BlockSpec(memory_space=pltpu.VMEM)
    hbm = pl.BlockSpec(memory_space=pl.ANY)
    dma = pltpu.SemaphoreType.DMA
    return pl.pallas_call(
        kernel,
        out_shape=jax.ShapeDtypeStruct(tokens.shape, BF),
        in_specs=[vmem, vmem, vmem, hbm, hbm, hbm],
        out_specs=vmem,
        scratch_shapes=[
            pltpu.VMEM((2 * half, hid), BF),
            pltpu.VMEM((2 * half, hid), BF),
            pltpu.VMEM((2 * hid, half), BF),
            pltpu.VMEM((n, 512, CW), BF),
            pltpu.VMEM((n, 2, 4, 80, CW), BF),
            pltpu.VMEM((n, 2, 4, 80, CW), BF),
            pltpu.VMEM((n, 2, 4, 80, CW), BF),
            pltpu.VMEM((2, 3, 640, hid), F32),
            pltpu.VMEM((3, 2, 640, hid), BF),
            pltpu.VMEM((n, 2, 4, 80, CW), BF),
            pltpu.VMEM((n, 3, 128, CW), BF),
            pltpu.VMEM((n, 3, 32, CW), BF),
            pltpu.VMEM((n, 128, CW), BF),
            pltpu.VMEM((3, 4, 4, 16, 128), F32),
            pltpu.VMEM((3, 2, 320, 256), BF),
            pltpu.VMEM((2, 3, 2, 256, 320), BF),
            dma((6, n, 3)),
            dma((6, n, 3)),
            dma((2, 3, 3)),
            dma((2, 3, 3)),
            dma((n,)),
            dma((n,)),
            dma((3,)),
            dma((3,)),
            dma((3,)),
            dma,
            dma,
        ],
        compiler_params=pltpu.CompilerParams(
            collective_id=0, has_side_effects=True, vmem_limit_bytes=64 * 1024 * 1024 - 512 * 1024
        ),
    )(tokens, info, perm, w_gate, w_up, w_down)


def solution(mesh):
    in_specs = (
        P("dev", "group"),
        P("dev", None),
        P("dev", None),
        P(),
        P("dev", None, "group"),
        P("dev", None, "group"),
        P("dev", "group", None),
    )
    out_specs = P("dev", "group")
    return jax.shard_map(body, mesh=mesh, in_specs=in_specs, out_specs=out_specs, check_vma=False)
```

```python
import jax
import jax.numpy as jnp
import numpy as np
from jax import lax
from jax.experimental import pallas as pl
from jax.experimental.pallas import tpu as pltpu
from jax.sharding import PartitionSpec as P

MESH = pl.DeviceIdType.MESH
BF = jnp.bfloat16
F32 = jnp.float32
CW = 512
EARLY = 2
COMBINE = 3
FIRST = 5
PACE = (5, 9, 12)
MAIN, REST = 8, 2
A_AG, B_AG, B_ON, C_OUT, C_BACK, B_RS, A_RS = range(7)


def place_of(q, rho):
    a, b, c = q[rho], q[(rho + 2) % 3], q[(rho + 1) % 3]
    return sum(q) % 2, c, b * 2 + a // 2


def main_row(q, rho):
    h, c, at = place_of(q, rho)
    return (h * 4 + c) * 80 + at * MAIN


def rest_matrices():
    mats = np.zeros((2, 3, 2, 64, 64), np.float32)
    for rho in range(3):
        for q in np.ndindex(4, 4, 4):
            h, c, at = place_of(q, rho)
            _, c0, at0 = place_of(q, 0)
            for j in range(REST):
                mats[0, rho, h, c0 * 16 + at0 * 2 + j, c * 16 + at * 2 + j] = 1
    mats[1] = np.swapaxes(mats[0], -1, -2)
    return mats


def dot(x, y):
    return jnp.dot(x, y, preferred_element_type=F32)


def kernel(
    tok, routes, weights_in, placement, perm, wg_hbm, wu_hbm, wd_hbm, out,
    WG, WU, WD, B, SB, X, XP, acc, HR, RB, RSB, RA, QB, IB, SEL, WT, info,
    ss, rs, iss, irs, ess, ers, hss, hrs, wsem, dss, drs,
):
    g = lax.axis_index("group")
    dev = lax.axis_index("dev")
    n = B.shape[0]
    half = n * CW

    def stride(ax):
        return lax.div(32 - 33 * ax + 9 * ax * ax, 2)

    def coord(ax):
        return lax.rem(lax.div(dev, stride(ax)), 4)

    def peer(ax, k):
        at = coord(ax)
        return dev + (lax.rem(at + k, 4) - at) * stride(ax)

    def axes(slot, core):
        rho = lax.rem(slot + core, 3)
        return rho, lax.rem(rho + 2, 3), lax.rem(rho + 1, 3)

    def remote(src, dst, s, r, ax, k):
        return pltpu.make_async_remote_copy(
            src, dst, s, r, device_id={"dev": peer(ax, k)}, device_id_type=MESH
        )

    def across(src, dst, s, r):
        return pltpu.make_async_remote_copy(
            src, dst, s, r, device_id={"group": 1 - g}, device_id_type=MESH
        )

    def block(i, size):
        return pl.ds(pl.multiple_of(i * size, size), size)

    parity = lax.rem(coord(0) + coord(1) + coord(2), 2)

    def a_ag(i, k):
        a, b, c = axes(lax.rem(i, 3), g)
        here = B.at[i, parity, block(coord(b) * 2 + lax.div(coord(a), 2), 32)]
        sems = (A_AG, i, 0, k - 1)
        return remote(tok.at[:, block(i, CW)], here, ss.at[sems], rs.at[sems], a, k)

    def b_ag(i, h, k):
        a, b, c = axes(lax.rem(i, 3), g)
        here = B.at[i, h, block(coord(b), 64)]
        sems = (B_AG, i, h, k - 1)
        return remote(here, here, ss.at[sems], rs.at[sems], b, k)

    def b_on(i, h, k):
        a, b, c = axes(lax.rem(i, 3), g)
        here = B.at[i, h, block(lax.rem(coord(b) + 4 - k, 4) * 2 + (k - 1) // 2, 32)]
        sems = (B_ON, i, h, k - 1)
        return remote(here, here, ss.at[sems], rs.at[sems], b, k)

    def c_out(i, h, k):
        a, b, c = axes(lax.rem(i, 3), g)
        to = lax.rem(coord(c) + k, 4)
        sems = (C_OUT, i, h, k - 1)
        return remote(SB.at[i, h, to], X.at[i, h, coord(c)], ss.at[sems], rs.at[sems], c, k)

    def c_back(i, h, k):
        a, b, c = axes(lax.rem(i, 3), g)
        to = lax.rem(coord(c) + k, 4)
        sems = (C_BACK, i, h, k - 1)
        return remote(SB.at[i, h, to], RB.at[i, h, coord(c)], ss.at[sems], rs.at[sems], c, k)

    def b_rs(i, h, k):
        a, b, c = axes(lax.rem(i, 3), g)
        to = lax.rem(coord(b) + k, 4)
        sems = (B_RS, i, h, k - 1)
        return remote(B.at[i, h, block(to, 64)], RSB.at[i, h, k - 1], ss.at[sems], rs.at[sems], b, k)

    def a_rs(i, k):
        a, b, c = axes(lax.rem(i, 3), g)
        to = lax.div(lax.rem(coord(a) + k, 4), 2)
        h = parity if k == 2 else 1 - parity
        sems = (A_RS, i, 0, k - 1)
        return remote(QB.at[i, h, block(to, 32)], RA.at[i, k - 1], ss.at[sems], rs.at[sems], a, k)

    def info_a(r, k):
        a, b, c = axes(r, g)
        return remote(info, IB.at[r, coord(b), coord(a)], iss.at[0, r, k - 1], irs.at[0, r, k - 1], a, k)

    def info_b(r, k):
        a, b, c = axes(r, g)
        here = IB.at[r, coord(b)]
        return remote(here, here, iss.at[1, r, k - 1], irs.at[1, r, k - 1], b, k)

    def rows_across(i, h):
        return across(X.at[i, h], XP.at[i, h], ess.at[i, h], ers.at[i, h])

    def hidden_across(rho, h):
        part = HR.at[rho, g, pl.ds(h * 320, 320)]
        return across(part, part, hss.at[rho, h], hrs.at[rho, h])

    def in_half(h, same, other):
        pl.when(parity == h)(lambda: [fn() for fn in same] and None)
        pl.when(parity != h)(lambda: [fn() for fn in other] and None)

    def loop(start, stop, fn):
        def step(i, carry):
            fn(i)
            return carry

        lax.fori_loop(start, stop, step, 0)

    def every(fn):
        loop(0, n, fn)

    def of(fn, h):
        return lambda i: fn(i, h)

    def stages(*work):
        def step(s):
            for fn, lag, *first in work:
                start = lag + (first[0] if first else 0)
                pl.when((s >= start) & (s < n + lag))(lambda fn=fn, lag=lag: fn(s - lag))

        loop(0, n + max(w[1] for w in work), step)

    bar = pltpu.get_barrier_semaphore()
    for ax in range(3):
        for k in (1, 2, 3):
            pl.semaphore_signal(bar, inc=1, device_id={"dev": peer(ax, k)}, device_id_type=MESH)
    pl.semaphore_signal(bar, inc=1, device_id={"group": 1 - g}, device_id_type=MESH)
    dest = jnp.zeros(routes.shape, jnp.int32)
    for e in range(placement.shape[0]):
        dest = jnp.where(routes[...] == e, placement[e], dest)
    info[0:8, :] = jnp.concatenate([dest.astype(F32)] * 4, axis=1)
    info[8:16, :] = jnp.concatenate([weights_in[...]] * 4, axis=1)
    acc[...] = jnp.zeros_like(acc)
    pl.semaphore_wait(bar, 10)

    for r in range(3):
        a, b, c = axes(r, g)
        for k in (1, 2, 3):
            info_a(r, k).start()
        IB[r, coord(b), coord(a)] = info[...]

    @every
    def _(i):
        a, b, c = axes(lax.rem(i, 3), g)
        for k in (1, 2, 3):
            a_ag(i, k).start()
        B[i, parity, block(coord(b) * 2 + lax.div(coord(a), 2), 32), :] = tok[:, block(i, CW)]

    wg_copy = pltpu.make_async_copy(wg_hbm.at[0], WG, wsem.at[0])
    wu_copy = pltpu.make_async_copy(wu_hbm.at[0], WU, wsem.at[1])
    hid = WG.shape[1]
    wd_copy = pltpu.make_async_copy(wd_hbm.at[0, :, block(g, half)], WD.at[block(g, hid)], wsem.at[2])
    wd_across = across(wd_hbm.at[0, :, block(1 - g, half)], WD.at[block(g, hid)], dss, drs)
    wg_copy.start()
    wu_copy.start()
    wd_copy.start()
    wd_across.start()

    def second_axis(i, h):
        in_half(
            h,
            [lambda: a_ag(i, 2).wait_recv()],
            [lambda: a_ag(i, 1).wait_recv(), lambda: a_ag(i, 3).wait_recv()],
        )
        for k in (1, 3):
            b_ag(i, h, k).start()

    def pass_on(i, h):
        for k in (1, 3):
            b_ag(i, h, k).wait_recv()
            b_on(i, h, k).start()

    for r in range(3):
        for k in (1, 2, 3):
            info_a(r, k).wait_recv()
        for k in (1, 2, 3):
            info_b(r, k).start()

    stages((of(second_axis, 0), 0))
    stages((of(second_axis, 1), 0), (of(pass_on, 0), 0))

    lane = lax.broadcasted_iota(jnp.int32, (8, 128), 1)
    seg_mask = [(lane >= 32 * a) & (lane < 32 * a + 32) for a in range(4)]
    lane1 = lax.broadcasted_iota(jnp.int32, (16, 128), 1)
    seg16 = sum(jnp.where(lane1 >= 32 * a, 1, 0) for a in (1, 2, 3))
    row1 = lax.broadcasted_iota(jnp.int32, (16, 128), 0)
    odd = jnp.where(((row1 >= 4) & (row1 < 8)) | (row1 >= 12), 1, 0)
    src8 = (odd * 4 + seg16).astype(F32)
    ti = lax.broadcasted_iota(jnp.int32, (128, 128), 0)
    tj = lax.broadcasted_iota(jnp.int32, (128, 128), 1)
    start_j = sum(jnp.where(tj >= 32 * a, 32, 0) for a in (1, 2, 3))
    before = jnp.where((ti < tj) & (ti >= start_j), 1.0, 0.0).astype(BF)
    iota_q = lax.broadcasted_iota(jnp.int32, (80, 128), 0).astype(F32)
    iota_k = lax.broadcasted_iota(jnp.int32, (128, 320), 1).astype(F32)

    for r in range(3):
        a_ax, b_ax, c_ax = axes(r, g)
        for k in (1, 2, 3):
            info_b(r, k).wait_recv()
        hits, weights = [], []
        for pair in range(4):
            h, first = pair // 2, pair % 2 * 2
            from_a = [
                2 * (s % 2) + lax.rem(h + first + s // 2 + coord(c_ax), 2) for s in range(4)
            ]
            dest = sum(jnp.where(seg_mask[s], IB[r, first + s // 2, from_a[s], 0:8, :], 0.0) for s in range(4))
            wts = sum(jnp.where(seg_mask[s], IB[r, first + s // 2, from_a[s], 8:16, :], 0.0) for s in range(4))
            for d in range(4):
                target = (dev + (d - coord(c_ax)) * stride(c_ax)).astype(F32)
                hit = dest == target
                hits.append(jnp.sum(jnp.where(hit, 1.0, 0.0), axis=0, keepdims=True))
                weights.append(jnp.sum(jnp.where(hit, wts, 0.0), axis=0, keepdims=True))
        hits = jnp.concatenate(hits, axis=0)
        weights = jnp.concatenate(weights, axis=0)
        rank = dot(hits.astype(BF), before)
        place = jnp.where(rank < MAIN, src8 * MAIN + rank, 64 + src8 * REST + (rank - MAIN))
        place = jnp.where(hits > 0, place, -1000.0)
        fill = jnp.zeros((112, 128), F32)
        place_t = jnp.transpose(jnp.concatenate([place, fill], axis=0))
        weights_t = jnp.transpose(jnp.concatenate([weights, fill], axis=0))
        for pair in range(4):
            total = jnp.zeros((128, 320), F32)
            cols = slice(pair % 2 * 128, pair % 2 * 128 + 128)
            for d in range(4):
                at = pair * 4 + d
                SEL[r, pair // 2, d * 80 : d * 80 + 80, cols] = jnp.where(
                    iota_q == place[at : at + 1, :], 1.0, 0.0
                ).astype(BF)
                total = total + jnp.where(
                    iota_k == place_t[:, at : at + 1] + 80.0 * d, weights_t[:, at : at + 1], 0.0
                )
            WT[r, pair // 2, cols, :] = total.astype(BF)

    def select(i, h):
        r = lax.rem(i, 3)
        a, b, c = axes(r, g)
        for k in (1, 3):
            b_on(i, h, k).wait_recv()
        SB[i, h] = dot(SEL[r, h], B[i, h]).astype(BF).reshape(4, 80, CW)
        for k in (1, 2, 3):
            c_out(i, h, k).start()
        X[i, h, coord(c)] = SB[i, h, coord(c)]

    def multiply(rows_ref, i, h, core):
        rho, _, _ = axes(lax.rem(i, 3), core)
        rows = rows_ref[i, h].reshape(320, CW)
        depth = pl.ds(pl.multiple_of(core * half + i * CW, CW), CW)
        for w, weight in enumerate((WG, WU)):
            acc[w, rho, h * 320 : h * 320 + 320, :] += dot(rows, weight[depth, :])

    def arrived(i, h):
        rho, _, _ = axes(lax.rem(i, 3), g)
        for k in (1, 2, 3):
            c_out(i, h, k).wait_recv()
        rest = jnp.concatenate([X[i, h, c, 64:80, :] for c in range(4)], axis=0)
        rest = dot(perm[0, rho, h], rest).astype(BF)
        for c in range(4):
            X[i, h, c, 64:80, :] = rest[c * 16 : c * 16 + 16, :]
        rows_across(i, h).start()
        multiply(X, i, h, g)

    def crossed(i, h):
        rows_across(i, h).wait_recv()
        multiply(XP, i, h, 1 - g)

    def swiglu(gate, up):
        return gate / (1.0 + jnp.exp(-gate)) * up

    def hidden(h):
        own = [q for q in np.ndindex(4, 4, 4) if sum(q) % 2 == h]
        for q in own:
            rows = [slice(main_row(q, rho), main_row(q, rho) + MAIN) for rho in range(3)]
            gate = acc[0, 0, rows[0], :] + acc[0, 1, rows[1], :] + acc[0, 2, rows[2], :]
            up = acc[1, 0, rows[0], :] + acc[1, 1, rows[1], :] + acc[1, 2, rows[2], :]
            acc[0, 0, rows[0], :] = swiglu(gate, up)
        rest_at = [(h * 4 + c) * 80 + 64 for c in range(4)]
        for at in rest_at:
            rows = slice(at, at + 16)
            gate = acc[0, 0, rows, :] + acc[0, 1, rows, :] + acc[0, 2, rows, :]
            up = acc[1, 0, rows, :] + acc[1, 1, rows, :] + acc[1, 2, rows, :]
            acc[0, 0, rows, :] = swiglu(gate, up)

        rest = jnp.concatenate([acc[0, 0, at : at + 16, :] for at in rest_at], axis=0).astype(BF)
        for rho in range(3):
            for q in own:
                if q[rho] >= 2:
                    continue
                two = list(q)
                two[rho] += 2
                here = main_row(q, rho)
                one, other = main_row(q, 0), main_row(two, 0)
                HR[rho, g, here : here + 16, :] = jnp.concatenate(
                    [acc[0, 0, one : one + MAIN, :], acc[0, 0, other : other + MAIN, :]], axis=0
                ).astype(BF)
            turned = dot(perm[1, rho, h], rest).astype(BF)
            for c in range(4):
                HR[rho, g, rest_at[c] : rest_at[c] + 16, :] = turned[c * 16 : c * 16 + 16, :]
        for r in range(3):
            hidden_across(lax.rem(r + 1 - g, 3), h).start()

    def down(i, h):
        rho, _, c = axes(lax.rem(i, 3), g)
        for k in (1, 2, 3):
            c_out(i, h, k).wait_send()

        @pl.when(i < 3)
        def _():
            hidden_across(rho, h).wait_recv()

        rows = slice(h * 320, h * 320 + 320)
        cols = block(i, CW)
        both = jnp.concatenate([HR[rho, 0, rows, :], HR[rho, 1, rows, :]], axis=1)
        SB[i, h] = dot(both, WD[:, cols]).astype(BF).reshape(4, 80, CW)
        for k in (1, 2, 3):
            c_back(i, h, k).start()
        RB[i, h, coord(c)] = SB[i, h, coord(c)]

    def combine(i, h):
        r = lax.rem(i, 3)
        for k in (1, 2, 3):
            c_back(i, h, k).wait_recv()
        for k in (1, 3):
            b_ag(i, h, k).wait_send()
            b_on(i, h, k).wait_send()
        rows = RB[i, h].reshape(320, CW)
        B[i, h] = dot(WT[r, h], rows).astype(BF)
        for k in (1, 2, 3):
            b_rs(i, h, k).start()

    def first_axis(i, h):
        a, b, c = axes(lax.rem(i, 3), g)
        for k in (1, 2, 3):
            b_rs(i, h, k).wait_recv()
        total = B[i, h, block(coord(b), 64), :].astype(F32)
        for k in range(3):
            total = total + RSB[i, h, k].astype(F32)
        QB[i, h] = total.astype(BF)
        in_half(h, [lambda: a_rs(i, 2).start()], [lambda: a_rs(i, 1).start(), lambda: a_rs(i, 3).start()])

    def finish(i):
        a, b, c = axes(lax.rem(i, 3), g)
        for k in (1, 2, 3):
            a_rs(i, k).wait_recv()
        total = QB[i, parity, block(lax.div(coord(a), 2), 32), :].astype(F32)
        for k in range(3):
            total = total + RA[i, k].astype(F32)
        out[:, block(i, CW)] = total.astype(BF)

    stages((of(pass_on, 1), 0))
    stages((of(select, 0), 0))
    stages((of(select, 1), 0))
    wg_copy.wait()
    wu_copy.wait()
    stages((of(arrived, 0), 0), (of(crossed, 0), 1))
    hidden(0)
    wd_copy.wait()
    wd_across.wait()
    loop(0, EARLY, of(arrived, 1))
    stages((of(down, 0), 0))
    stages((of(arrived, 1), 0, EARLY), (of(crossed, 1), 1), (of(combine, 0), COMBINE))
    hidden(1)
    stages((of(down, 1), 0), (of(first_axis, 0), FIRST), (of(combine, 1), PACE[0]), (of(first_axis, 1), PACE[1]), (finish, PACE[2]))

    @every
    def _(i):
        for k in (1, 2, 3):
            a_ag(i, k).wait_send()
            a_rs(i, k).wait_send()
            for h in range(2):
                c_back(i, h, k).wait_send()
        for k in (1, 2, 3):
            for h in range(2):
                b_rs(i, h, k).wait_send()
        for h in range(2):
            rows_across(i, h).wait_send()

    for r in range(3):
        for k in (1, 2, 3):
            info_a(r, k).wait_send()
            info_b(r, k).wait_send()
        for h in range(2):
            hidden_across(r, h).wait_send()


def body(tokens, routes, route_weights, placement, w_gate, w_up, w_down):
    local_tokens, half = tokens.shape
    n = half // CW
    hid = w_gate.shape[2]
    perm = jnp.asarray(rest_matrices(), BF)
    vmem = pl.BlockSpec(memory_space=pltpu.VMEM)
    hbm = pl.BlockSpec(memory_space=pl.ANY)
    dma = pltpu.SemaphoreType.DMA
    return pl.pallas_call(
        kernel,
        out_shape=jax.ShapeDtypeStruct(tokens.shape, BF),
        in_specs=[vmem, vmem, vmem, pl.BlockSpec(memory_space=pltpu.SMEM), vmem, hbm, hbm, hbm],
        out_specs=vmem,
        scratch_shapes=[
            pltpu.VMEM((2 * half, hid), BF),
            pltpu.VMEM((2 * half, hid), BF),
            pltpu.VMEM((2 * hid, half), BF),
            pltpu.VMEM((n, 2, 256, CW), BF),
            pltpu.VMEM((n, 2, 4, 80, CW), BF),
            pltpu.VMEM((n, 2, 4, 80, CW), BF),
            pltpu.VMEM((n, 2, 4, 80, CW), BF),
            pltpu.VMEM((2, 3, 640, hid), F32),
            pltpu.VMEM((3, 2, 640, hid), BF),
            pltpu.VMEM((n, 2, 4, 80, CW), BF),
            pltpu.VMEM((n, 2, 3, 64, CW), BF),
            pltpu.VMEM((n, 3, 32, CW), BF),
            pltpu.VMEM((n, 2, 64, CW), BF),
            pltpu.VMEM((3, 4, 4, 16, 128), F32),
            pltpu.VMEM((3, 2, 320, 256), BF),
            pltpu.VMEM((3, 2, 256, 320), BF),
            pltpu.VMEM((16, 128), F32),
            dma((7, n, 2, 3)),
            dma((7, n, 2, 3)),
            dma((2, 3, 3)),
            dma((2, 3, 3)),
            dma((n, 2)),
            dma((n, 2)),
            dma((3, 2)),
            dma((3, 2)),
            dma((3,)),
            dma,
            dma,
        ],
        compiler_params=pltpu.CompilerParams(
            collective_id=0, has_side_effects=True, vmem_limit_bytes=64 * 1024 * 1024 - 512 * 1024
        ),
    )(tokens, routes.T, route_weights.T, placement, perm, w_gate, w_up, w_down)


def solution(mesh):
    in_specs = (
        P("dev", "group"),
        P("dev", None),
        P("dev", None),
        P(),
        P("dev", None, "group"),
        P("dev", None, "group"),
        P("dev", "group", None),
    )
    out_specs = P("dev", "group")
    return jax.shard_map(body, mesh=mesh, in_specs=in_specs, out_specs=out_specs, check_vma=False)
```

```python
import jax
import jax.numpy as jnp
import numpy as np
from jax import lax
from jax.experimental import pallas as pl
from jax.experimental.pallas import tpu as pltpu
from jax.sharding import PartitionSpec as P

MESH = pl.DeviceIdType.MESH
BF = jnp.bfloat16
F32 = jnp.float32
CW = 512
EARLY = 2
COMBINE = 3
FIRST = 6
SPLIT = 5
PACE = (6, 10, 13)
MAIN, REST = 8, 2
A_AG, B_AG, B_ON, C_OUT, C_BACK, B_RS, A_RS = range(7)


def place_of(q, rho):
    a, b, c = q[rho], q[(rho + 2) % 3], q[(rho + 1) % 3]
    return sum(q) % 2, c, b * 2 + a // 2


def main_row(q, rho):
    h, c, at = place_of(q, rho)
    return (h * 4 + c) * 80 + at * MAIN


def rest_matrices():
    mats = np.zeros((2, 3, 2, 64, 64), np.float32)
    for rho in range(3):
        for q in np.ndindex(4, 4, 4):
            h, c, at = place_of(q, rho)
            _, c0, at0 = place_of(q, 0)
            for j in range(REST):
                mats[0, rho, h, c0 * 16 + at0 * 2 + j, c * 16 + at * 2 + j] = 1
    mats[1] = np.swapaxes(mats[0], -1, -2)
    return mats


def dot(x, y):
    return jnp.dot(x, y, preferred_element_type=F32)


def kernel(
    tok, routes, weights_in, placement, perm, wg_hbm, wu_hbm, wd_hbm, out,
    WG, WU, WD, B, SB, X, XP, acc, HR, RB, RSB, RA, QB, IB, SEL, WT, info,
    ss, rs, iss, irs, ess, ers, hss, hrs, wsem, dss, drs,
):
    g = lax.axis_index("group")
    dev = lax.axis_index("dev")
    n = B.shape[0]
    half = n * CW

    place = (lax.div(dev, 16), lax.rem(lax.div(dev, 4), 4), lax.rem(dev, 4))

    def one_of(ax, first, second, third):
        return jnp.where(ax == 0, first, jnp.where(ax == 1, second, third))

    def stride(ax):
        return one_of(ax, 16, 4, 1)

    def coord(ax):
        return one_of(ax, *place)

    def peer(ax, k):
        at = coord(ax)
        return dev + (lax.rem(at + k, 4) - at) * stride(ax)

    def axes(slot, core):
        rho = slot + core
        rho = jnp.where(rho == 3, 0, rho)
        return rho, jnp.where(rho == 0, 2, rho - 1), jnp.where(rho == 2, 0, rho + 1)

    def remote(src, dst, s, r, ax, k):
        return pltpu.make_async_remote_copy(
            src, dst, s, r, device_id={"dev": peer(ax, k)}, device_id_type=MESH
        )

    def across(src, dst, s, r):
        return pltpu.make_async_remote_copy(
            src, dst, s, r, device_id={"group": 1 - g}, device_id_type=MESH
        )

    def block(i, size):
        return pl.ds(pl.multiple_of(i * size, size), size)

    parity = lax.rem(place[0] + place[1] + place[2], 2)

    def a_ag(i, k):
        a, b, c = axes(lax.rem(i, 3), g)
        here = B.at[i, parity, block(coord(b) * 2 + lax.div(coord(a), 2), 32)]
        return remote(tok.at[:, block(i, CW)], here, ss.at[A_AG, 0], rs.at[A_AG, i, parity], a, k)

    def b_ag(i, h, k):
        a, b, c = axes(lax.rem(i, 3), g)
        here = B.at[i, h, block(coord(b), 64)]
        sems = ss.at[B_AG, h], rs.at[B_AG, i, h]
        return remote(here, here, *sems, b, k)

    def b_on(i, h, k):
        a, b, c = axes(lax.rem(i, 3), g)
        here = B.at[i, h, block(lax.rem(coord(b) + 4 - k, 4) * 2 + (k - 1) // 2, 32)]
        sems = ss.at[B_ON, h], rs.at[B_ON, i, h]
        return remote(here, here, *sems, b, k)

    def c_out(i, h, k):
        a, b, c = axes(lax.rem(i, 3), g)
        to = lax.rem(coord(c) + k, 4)
        sems = ss.at[C_OUT, h], rs.at[C_OUT, i, h]
        return remote(SB.at[i, h, to], X.at[i, h, coord(c)], *sems, c, k)

    def c_back(i, h, k):
        a, b, c = axes(lax.rem(i, 3), g)
        to = lax.rem(coord(c) + k, 4)
        sems = ss.at[C_BACK, h], rs.at[C_BACK, i, h]
        return remote(SB.at[i, h, to], RB.at[i, h, coord(c)], *sems, c, k)

    def b_rs(i, h, k):
        a, b, c = axes(lax.rem(i, 3), g)
        to = lax.rem(coord(b) + k, 4)
        sems = ss.at[B_RS, h], rs.at[B_RS, i, h]
        return remote(B.at[i, h, block(to, 64)], RSB.at[i, h, k - 1], *sems, b, k)

    def a_rs(i, k):
        a, b, c = axes(lax.rem(i, 3), g)
        to = lax.div(lax.rem(coord(a) + k, 4), 2)
        h = parity if k == 2 else 1 - parity
        sems = ss.at[A_RS, 0], rs.at[A_RS, i, 0]
        return remote(QB.at[i, h, block(to, 32)], RA.at[i, k - 1], *sems, a, k)

    def info_a(r, k):
        a, b, c = axes(r, g)
        return remote(info, IB.at[r, coord(b), coord(a)], iss.at[0], irs.at[0, r], a, k)

    def info_b(r, k):
        a, b, c = axes(r, g)
        here = IB.at[r, coord(b)]
        return remote(here, here, iss.at[1], irs.at[1, r], b, k)

    def rows_across(i, h):
        return across(X.at[i, h], XP.at[i, h], ess, ers.at[i, h])

    def hidden_across(rho, h):
        part = HR.at[rho, g, pl.ds(h * 320, 320)]
        return across(part, part, hss, hrs.at[rho, h])

    def landed(all_of, sem):
        across(all_of, all_of, sem, sem).wait_recv()

    def sent(all_of, sem):
        across(all_of, all_of, sem, sem).wait_send()

    def in_half(h, same, other):
        pl.when(parity == h)(lambda: [fn() for fn in same] and None)
        pl.when(parity != h)(lambda: [fn() for fn in other] and None)

    def loop(start, stop, fn):
        def step(i, carry):
            fn(i)
            return carry

        lax.fori_loop(start, stop, step, 0)

    def every(fn):
        loop(0, n, fn)

    def of(fn, h):
        return lambda i: fn(i, h)

    def stages(*work):
        def step(s):
            for fn, lag, *span in work:
                first, last = span or (0, n)
                pl.when((s >= first + lag) & (s < last + lag))(lambda fn=fn, lag=lag: fn(s - lag))

        loop(0, max(lag + (span[1] if span else n) for _, lag, *span in work), step)

    bar = pltpu.get_barrier_semaphore()
    for ax in range(3):
        for k in (1, 2, 3):
            pl.semaphore_signal(bar, inc=1, device_id={"dev": peer(ax, k)}, device_id_type=MESH)
    pl.semaphore_signal(bar, inc=1, device_id={"group": 1 - g}, device_id_type=MESH)
    dest = jnp.zeros(routes.shape, jnp.int32)
    for e in range(placement.shape[0]):
        dest = jnp.where(routes[...] == e, placement[e], dest)
    info[0:8, :] = jnp.concatenate([dest.astype(F32)] * 4, axis=1)
    info[8:16, :] = jnp.concatenate([weights_in[...]] * 4, axis=1)
    pl.semaphore_wait(bar, 10)

    for r in range(3):
        a, b, c = axes(r, g)
        for k in (1, 2, 3):
            info_a(r, k).start()
        IB[r, coord(b), coord(a)] = info[...]

    @every
    def _(i):
        a, b, c = axes(lax.rem(i, 3), g)
        for k in (1, 2, 3):
            a_ag(i, k).start()
        B[i, parity, block(coord(b) * 2 + lax.div(coord(a), 2), 32), :] = tok[:, block(i, CW)]

    wg_copy = pltpu.make_async_copy(wg_hbm.at[0], WG, wsem.at[0])
    wu_copy = pltpu.make_async_copy(wu_hbm.at[0], WU, wsem.at[1])
    hid = WG.shape[1]
    wd_copy = pltpu.make_async_copy(wd_hbm.at[0, :, block(g, half)], WD.at[block(g, hid)], wsem.at[2])
    wd_across = across(wd_hbm.at[0, :, block(1 - g, half)], WD.at[block(g, hid)], dss, drs)
    wg_copy.start()
    wu_copy.start()
    wd_copy.start()
    wd_across.start()

    def second_axis(i, h):
        in_half(
            h,
            [lambda: landed(B.at[i, h, 0:32], rs.at[A_AG, i, h])],
            [lambda: landed(B.at[i, h, 0:64], rs.at[A_AG, i, h])],
        )
        for k in (1, 3):
            b_ag(i, h, k).start()

    def pass_on(i, h):
        landed(B.at[i, h, 0:128], rs.at[B_AG, i, h])
        for k in (1, 3):
            b_on(i, h, k).start()

    for r in range(3):
        landed(IB.at[r, 0, 0:3], irs.at[0, r])
        for k in (1, 2, 3):
            info_b(r, k).start()

    stages((of(second_axis, 0), 0))
    stages((of(second_axis, 1), 0), (of(pass_on, 0), 0))

    acc[...] = jnp.zeros_like(acc)

    lane = lax.broadcasted_iota(jnp.int32, (8, 128), 1)
    seg_mask = [(lane >= 32 * a) & (lane < 32 * a + 32) for a in range(4)]
    lane1 = lax.broadcasted_iota(jnp.int32, (16, 128), 1)
    seg16 = sum(jnp.where(lane1 >= 32 * a, 1, 0) for a in (1, 2, 3))
    row1 = lax.broadcasted_iota(jnp.int32, (16, 128), 0)
    odd = jnp.where(((row1 >= 4) & (row1 < 8)) | (row1 >= 12), 1, 0)
    src8 = (odd * 4 + seg16).astype(F32)
    ti = lax.broadcasted_iota(jnp.int32, (128, 128), 0)
    tj = lax.broadcasted_iota(jnp.int32, (128, 128), 1)
    start_j = sum(jnp.where(tj >= 32 * a, 32, 0) for a in (1, 2, 3))
    before = jnp.where((ti < tj) & (ti >= start_j), 1.0, 0.0).astype(BF)
    iota_q = lax.broadcasted_iota(jnp.int32, (80, 128), 0).astype(F32)
    iota_k = lax.broadcasted_iota(jnp.int32, (128, 320), 1).astype(F32)

    for r in range(3):
        a_ax, b_ax, c_ax = axes(r, g)
        landed(IB.at[r, 0:3], irs.at[1, r])
        hits, weights = [], []
        for pair in range(4):
            h, first = pair // 2, pair % 2 * 2
            from_a = [
                2 * (s % 2) + lax.rem(h + first + s // 2 + coord(c_ax), 2) for s in range(4)
            ]
            dest = sum(jnp.where(seg_mask[s], IB[r, first + s // 2, from_a[s], 0:8, :], 0.0) for s in range(4))
            wts = sum(jnp.where(seg_mask[s], IB[r, first + s // 2, from_a[s], 8:16, :], 0.0) for s in range(4))
            for d in range(4):
                target = (dev + (d - coord(c_ax)) * stride(c_ax)).astype(F32)
                hit = dest == target
                hits.append(jnp.sum(jnp.where(hit, 1.0, 0.0), axis=0, keepdims=True))
                weights.append(jnp.sum(jnp.where(hit, wts, 0.0), axis=0, keepdims=True))
        hits = jnp.concatenate(hits, axis=0)
        weights = jnp.concatenate(weights, axis=0)
        rank = dot(hits.astype(BF), before)
        at_row = jnp.where(rank < MAIN, src8 * MAIN + rank, 64 + src8 * REST + (rank - MAIN))
        at_row = jnp.where(hits > 0, at_row, -1000.0)
        fill = jnp.zeros((112, 128), F32)
        place_t = jnp.transpose(jnp.concatenate([at_row, fill], axis=0))
        weights_t = jnp.transpose(jnp.concatenate([weights, fill], axis=0))
        for pair in range(4):
            total = jnp.zeros((128, 320), F32)
            cols = slice(pair % 2 * 128, pair % 2 * 128 + 128)
            for d in range(4):
                at = pair * 4 + d
                SEL[r, pair // 2, d * 80 : d * 80 + 80, cols] = jnp.where(
                    iota_q == at_row[at : at + 1, :], 1.0, 0.0
                ).astype(BF)
                total = total + jnp.where(
                    iota_k == place_t[:, at : at + 1] + 80.0 * d, weights_t[:, at : at + 1], 0.0
                )
            WT[r, pair // 2, cols, :] = total.astype(BF)

    def select(i, h):
        r = lax.rem(i, 3)
        a, b, c = axes(r, g)
        landed(B.at[i, h, 0:64], rs.at[B_ON, i, h])
        SB[i, h] = dot(SEL[r, h], B[i, h]).astype(BF).reshape(4, 80, CW)
        for k in (1, 2, 3):
            c_out(i, h, k).start()
        X[i, h, coord(c)] = SB[i, h, coord(c)]

    def multiply(rows_ref, i, h, core):
        rho, _, _ = axes(lax.rem(i, 3), core)
        rows = rows_ref[i, h].reshape(320, CW)
        depth = pl.ds(pl.multiple_of(core * half + i * CW, CW), CW)
        for w, weight in enumerate((WG, WU)):
            acc[w, rho, h * 320 : h * 320 + 320, :] += dot(rows, weight[depth, :])

    def arrived(i, h):
        rho, _, _ = axes(lax.rem(i, 3), g)
        landed(X.at[i, h, 0:3], rs.at[C_OUT, i, h])
        rest = jnp.concatenate([X[i, h, c, 64:80, :] for c in range(4)], axis=0)
        rest = dot(perm[0, rho, h], rest).astype(BF)
        for c in range(4):
            X[i, h, c, 64:80, :] = rest[c * 16 : c * 16 + 16, :]
        rows_across(i, h).start()
        multiply(X, i, h, g)

    def crossed(i, h):
        rows_across(i, h).wait_recv()
        multiply(XP, i, h, 1 - g)

    def swiglu(gate, up):
        return gate / (1.0 + jnp.exp(-gate)) * up

    def hidden(h):
        own = [q for q in np.ndindex(4, 4, 4) if sum(q) % 2 == h]
        for q in own:
            rows = [slice(main_row(q, rho), main_row(q, rho) + MAIN) for rho in range(3)]
            gate = acc[0, 0, rows[0], :] + acc[0, 1, rows[1], :] + acc[0, 2, rows[2], :]
            up = acc[1, 0, rows[0], :] + acc[1, 1, rows[1], :] + acc[1, 2, rows[2], :]
            acc[0, 0, rows[0], :] = swiglu(gate, up)
        rest_at = [(h * 4 + c) * 80 + 64 for c in range(4)]
        for at in rest_at:
            rows = slice(at, at + 16)
            gate = acc[0, 0, rows, :] + acc[0, 1, rows, :] + acc[0, 2, rows, :]
            up = acc[1, 0, rows, :] + acc[1, 1, rows, :] + acc[1, 2, rows, :]
            acc[0, 0, rows, :] = swiglu(gate, up)

        rest = jnp.concatenate([acc[0, 0, at : at + 16, :] for at in rest_at], axis=0).astype(BF)
        for rho in range(3):
            for q in own:
                if q[rho] >= 2:
                    continue
                two = list(q)
                two[rho] += 2
                here = main_row(q, rho)
                one, other = main_row(q, 0), main_row(two, 0)
                HR[rho, g, here : here + 16, :] = jnp.concatenate(
                    [acc[0, 0, one : one + MAIN, :], acc[0, 0, other : other + MAIN, :]], axis=0
                ).astype(BF)
            turned = dot(perm[1, rho, h], rest).astype(BF)
            for c in range(4):
                HR[rho, g, rest_at[c] : rest_at[c] + 16, :] = turned[c * 16 : c * 16 + 16, :]
        for r in range(3):
            hidden_across(lax.rem(r + 1 - g, 3), h).start()

    def down(i, h):
        rho, _, c = axes(lax.rem(i, 3), g)

        @pl.when(i < 3)
        def _():
            hidden_across(rho, h).wait_recv()

        rows = slice(h * 320, h * 320 + 320)
        cols = block(i, CW)
        both = jnp.concatenate([HR[rho, 0, rows, :], HR[rho, 1, rows, :]], axis=1)
        SB[i, h] = dot(both, WD[:, cols]).astype(BF).reshape(4, 80, CW)
        for k in (1, 2, 3):
            c_back(i, h, k).start()
        RB[i, h, coord(c)] = SB[i, h, coord(c)]

    def combine(i, h):
        r = lax.rem(i, 3)
        landed(RB.at[i, h, 0:3], rs.at[C_BACK, i, h])
        rows = RB[i, h].reshape(320, CW)
        B[i, h] = dot(WT[r, h], rows).astype(BF)
        for k in (1, 2, 3):
            b_rs(i, h, k).start()

    def first_axis(i, h):
        a, b, c = axes(lax.rem(i, 3), g)
        landed(RSB.at[i, h], rs.at[B_RS, i, h])
        total = B[i, h, block(coord(b), 64), :].astype(F32)
        for k in range(3):
            total = total + RSB[i, h, k].astype(F32)
        QB[i, h] = total.astype(BF)
        in_half(h, [lambda: a_rs(i, 2).start()], [lambda: a_rs(i, 1).start(), lambda: a_rs(i, 3).start()])

    def finish(i):
        a, b, c = axes(lax.rem(i, 3), g)
        landed(RA.at[i], rs.at[A_RS, i, 0])
        total = QB[i, parity, block(lax.div(coord(a), 2), 32), :].astype(F32)
        for k in range(3):
            total = total + RA[i, k].astype(F32)
        out[:, block(i, CW)] = total.astype(BF)

    stages((of(pass_on, 1), 0))
    stages((of(select, 0), 0))
    stages((of(select, 1), 0))
    wg_copy.wait()
    wu_copy.wait()
    stages((of(arrived, 0), 0), (of(crossed, 0), 1))
    hidden(0)
    wd_copy.wait()
    wd_across.wait()
    loop(0, EARLY, of(arrived, 1))
    sent(X.at[:, 0, 0:3], ss.at[C_OUT, 0])
    stages((of(down, 0), 0))
    for h in range(2):
        sent(B.at[:, h, 0:128], ss.at[B_AG, h])
        sent(B.at[:, h, 0:64], ss.at[B_ON, h])
    stages((of(arrived, 1), 0, EARLY, n), (of(crossed, 1), 1), (of(combine, 0), COMBINE, 0, SPLIT))
    hidden(1)
    loop(SPLIT, n, of(combine, 0))
    sent(X.at[:, 1, 0:3], ss.at[C_OUT, 1])
    stages((of(down, 1), 0), (of(first_axis, 0), FIRST), (of(combine, 1), PACE[0]), (of(first_axis, 1), PACE[1]), (finish, PACE[2]))

    sent(B.at[:, 0, 0:96], ss.at[A_AG, 0])
    for h in range(2):
        sent(RB.at[:, h, 0:3], ss.at[C_BACK, h])
        sent(RSB.at[:, h], ss.at[B_RS, h])
    sent(RA, ss.at[A_RS, 0])
    sent(XP, ess)
    sent(HR.at[:, 0], hss)
    sent(IB.at[:, 0, 0:3], iss.at[0])
    sent(IB.at[:, 0:3], iss.at[1])


def body(tokens, routes, route_weights, placement, w_gate, w_up, w_down):
    local_tokens, half = tokens.shape
    n = half // CW
    hid = w_gate.shape[2]
    perm = jnp.asarray(rest_matrices(), BF)
    vmem = pl.BlockSpec(memory_space=pltpu.VMEM)
    hbm = pl.BlockSpec(memory_space=pl.ANY)
    dma = pltpu.SemaphoreType.DMA
    return pl.pallas_call(
        kernel,
        out_shape=jax.ShapeDtypeStruct(tokens.shape, BF),
        in_specs=[vmem, vmem, vmem, pl.BlockSpec(memory_space=pltpu.SMEM), vmem, hbm, hbm, hbm],
        out_specs=vmem,
        scratch_shapes=[
            pltpu.VMEM((2 * half, hid), BF),
            pltpu.VMEM((2 * half, hid), BF),
            pltpu.VMEM((2 * hid, half), BF),
            pltpu.VMEM((n, 2, 256, CW), BF),
            pltpu.VMEM((n, 2, 4, 80, CW), BF),
            pltpu.VMEM((n, 2, 4, 80, CW), BF),
            pltpu.VMEM((n, 2, 4, 80, CW), BF),
            pltpu.VMEM((2, 3, 640, hid), F32),
            pltpu.VMEM((3, 2, 640, hid), BF),
            pltpu.VMEM((n, 2, 4, 80, CW), BF),
            pltpu.VMEM((n, 2, 3, 64, CW), BF),
            pltpu.VMEM((n, 3, 32, CW), BF),
            pltpu.VMEM((n, 2, 64, CW), BF),
            pltpu.VMEM((3, 4, 4, 16, 128), F32),
            pltpu.VMEM((3, 2, 320, 256), BF),
            pltpu.VMEM((3, 2, 256, 320), BF),
            pltpu.VMEM((16, 128), F32),
            dma((7, 2)),
            dma((7, n, 2)),
            dma((2,)),
            dma((2, 3)),
            dma,
            dma((n, 2)),
            dma,
            dma((3, 2)),
            dma((3,)),
            dma,
            dma,
        ],
        compiler_params=pltpu.CompilerParams(
            collective_id=0, has_side_effects=True, vmem_limit_bytes=64 * 1024 * 1024 - 512 * 1024
        ),
    )(tokens, routes.T, route_weights.T, placement, perm, w_gate, w_up, w_down)


def solution(mesh):
    in_specs = (
        P("dev", "group"),
        P("dev", None),
        P("dev", None),
        P(),
        P("dev", None, "group"),
        P("dev", None, "group"),
        P("dev", "group", None),
    )
    out_specs = P("dev", "group")
    return jax.shard_map(body, mesh=mesh, in_specs=in_specs, out_specs=out_specs, check_vma=False)
```

```python
import jax
import jax.numpy as jnp
import numpy as np
from jax import lax
from jax.experimental import pallas as pl
from jax.experimental.pallas import tpu as pltpu
from jax.sharding import PartitionSpec as P

MESH = pl.DeviceIdType.MESH
BF = jnp.bfloat16
F32 = jnp.float32
CW = 512
EARLY = 2
COMBINE = 3
FIRST = 7
SPLIT = 5
PACE = (7, 11, 14)
MAIN, REST = 8, 2
A_AG, B_AG, B_ON, C_OUT, C_BACK, B_RS, A_RS = range(7)


def place_of(q, rho):
    a, b, c = q[rho], q[(rho + 2) % 3], q[(rho + 1) % 3]
    return sum(q) % 2, c, b * 2 + a // 2


def main_row(q, rho):
    h, c, at = place_of(q, rho)
    return (h * 4 + c) * 80 + at * MAIN


def rest_matrices():
    mats = np.zeros((2, 3, 2, 64, 64), np.float32)
    for rho in range(3):
        for q in np.ndindex(4, 4, 4):
            h, c, at = place_of(q, rho)
            _, c0, at0 = place_of(q, 0)
            for j in range(REST):
                mats[0, rho, h, c0 * 16 + at0 * 2 + j, c * 16 + at * 2 + j] = 1
    mats[1] = np.swapaxes(mats[0], -1, -2)
    return mats


def dot(x, y):
    return jnp.dot(x, y, preferred_element_type=F32)


def kernel(
    tok, routes, weights_in, placement, perm, wg_hbm, wu_hbm, wd_hbm, out,
    WG, WU, WD, B, SB, X, XP, acc, HR, RB, RSB, RA, QB, IB, SEL, WT, info,
    ss, rs, iss, irs, ess, ers, hss, hrs, wsem, dss, drs,
):
    g = lax.axis_index("group")
    dev = lax.axis_index("dev")
    n = B.shape[0]
    half = n * CW

    place = (lax.div(dev, 16), lax.rem(lax.div(dev, 4), 4), lax.rem(dev, 4))

    def one_of(ax, first, second, third):
        return jnp.where(ax == 0, first, jnp.where(ax == 1, second, third))

    def stride(ax):
        return one_of(ax, 16, 4, 1)

    def coord(ax):
        return one_of(ax, *place)

    def peer(ax, k):
        at = coord(ax)
        return dev + (lax.rem(at + k, 4) - at) * stride(ax)

    def axes(slot, core):
        rho = slot + core
        rho = jnp.where(rho == 3, 0, rho)
        return rho, jnp.where(rho == 0, 2, rho - 1), jnp.where(rho == 2, 0, rho + 1)

    def remote(src, dst, s, r, ax, k):
        return pltpu.make_async_remote_copy(
            src, dst, s, r, device_id={"dev": peer(ax, k)}, device_id_type=MESH
        )

    def across(src, dst, s, r):
        return pltpu.make_async_remote_copy(
            src, dst, s, r, device_id={"group": 1 - g}, device_id_type=MESH
        )

    def block(i, size):
        return pl.ds(pl.multiple_of(i * size, size), size)

    parity = lax.rem(place[0] + place[1] + place[2], 2)

    def a_ag(i, k):
        a, b, c = axes(lax.rem(i, 3), g)
        here = B.at[i, parity, block(coord(b) * 2 + lax.div(coord(a), 2), 32)]
        return remote(tok.at[:, block(i, CW)], here, ss.at[A_AG, 0], rs.at[A_AG, i, parity], a, k)

    def b_ag(i, h, k):
        a, b, c = axes(lax.rem(i, 3), g)
        here = B.at[i, h, block(coord(b), 64)]
        sems = ss.at[B_AG, h], rs.at[B_AG, i, h]
        return remote(here, here, *sems, b, k)

    def b_on(i, h, k):
        a, b, c = axes(lax.rem(i, 3), g)
        here = B.at[i, h, block(lax.rem(coord(b) + 4 - k, 4) * 2 + (k - 1) // 2, 32)]
        sems = ss.at[B_ON, h], rs.at[B_ON, i, h]
        return remote(here, here, *sems, b, k)

    def c_out(i, h, k):
        a, b, c = axes(lax.rem(i, 3), g)
        to = lax.rem(coord(c) + k, 4)
        sems = ss.at[C_OUT, h], rs.at[C_OUT, i, h]
        return remote(SB.at[i, h, to], X.at[i, h, coord(c)], *sems, c, k)

    def c_back(i, h, k):
        a, b, c = axes(lax.rem(i, 3), g)
        to = lax.rem(coord(c) + k, 4)
        sems = ss.at[C_BACK, h], rs.at[C_BACK, i, h]
        return remote(SB.at[i, h, to], RB.at[i, h, coord(c)], *sems, c, k)

    def b_rs(i, h, k):
        a, b, c = axes(lax.rem(i, 3), g)
        to = lax.rem(coord(b) + k, 4)
        sems = ss.at[B_RS, h], rs.at[B_RS, i, h]
        return remote(B.at[i, h, block(to, 64)], RSB.at[i, h, k - 1], *sems, b, k)

    def a_rs(i, k):
        a, b, c = axes(lax.rem(i, 3), g)
        to = lax.div(lax.rem(coord(a) + k, 4), 2)
        h = parity if k == 2 else 1 - parity
        sems = ss.at[A_RS, 0], rs.at[A_RS, i, 0]
        return remote(QB.at[i, h, block(to, 32)], RA.at[i, k - 1], *sems, a, k)

    def info_a(r, k):
        a, b, c = axes(r, g)
        return remote(info, IB.at[r, coord(b), coord(a)], iss.at[0], irs.at[0, r], a, k)

    def info_b(r, k):
        a, b, c = axes(r, g)
        here = IB.at[r, coord(b)]
        return remote(here, here, iss.at[1], irs.at[1, r], b, k)

    def rows_across(i, h):
        return across(X.at[i, h], XP.at[i, h], ess, ers.at[i, h])

    def hidden_across(rho, h):
        part = HR.at[rho, g, pl.ds(h * 320, 320)]
        return across(part, part, hss, hrs.at[rho, h])

    def landed(all_of, sem):
        across(all_of, all_of, sem, sem).wait_recv()

    def sent(all_of, sem):
        across(all_of, all_of, sem, sem).wait_send()

    def in_half(h, same, other):
        pl.when(parity == h)(lambda: [fn() for fn in same] and None)
        pl.when(parity != h)(lambda: [fn() for fn in other] and None)

    def loop(start, stop, fn):
        def step(i, carry):
            fn(i)
            return carry

        lax.fori_loop(start, stop, step, 0)

    def every(fn):
        loop(0, n, fn)

    def of(fn, h):
        return lambda i: fn(i, h)

    def stages(*work):
        def step(s):
            for fn, lag, *span in work:
                first, last = span or (0, n)
                pl.when((s >= first + lag) & (s < last + lag))(lambda fn=fn, lag=lag: fn(s - lag))

        loop(0, max(lag + (span[1] if span else n) for _, lag, *span in work), step)

    bar = pltpu.get_barrier_semaphore()
    for ax in range(3):
        for k in (1, 2, 3):
            pl.semaphore_signal(bar, inc=1, device_id={"dev": peer(ax, k)}, device_id_type=MESH)
    pl.semaphore_signal(bar, inc=1, device_id={"group": 1 - g}, device_id_type=MESH)
    dest = jnp.zeros(routes.shape, jnp.int32)
    for e in range(placement.shape[0]):
        dest = jnp.where(routes[...] == e, placement[e], dest)
    info[0:8, :] = jnp.concatenate([dest.astype(F32)] * 4, axis=1)
    info[8:16, :] = jnp.concatenate([weights_in[...]] * 4, axis=1)
    pl.semaphore_wait(bar, 10)

    for r in range(3):
        a, b, c = axes(r, g)
        for k in (1, 2, 3):
            info_a(r, k).start()
        IB[r, coord(b), coord(a)] = info[...]

    @every
    def _(i):
        a, b, c = axes(lax.rem(i, 3), g)
        for k in (1, 2, 3):
            a_ag(i, k).start()
        B[i, parity, block(coord(b) * 2 + lax.div(coord(a), 2), 32), :] = tok[:, block(i, CW)]

    wg_copy = pltpu.make_async_copy(wg_hbm.at[0], WG, wsem.at[0])
    wu_copy = pltpu.make_async_copy(wu_hbm.at[0], WU, wsem.at[1])
    hid = WG.shape[1]
    wd_copy = pltpu.make_async_copy(wd_hbm.at[0, :, block(g, half)], WD.at[block(g, hid)], wsem.at[2])
    wd_across = across(wd_hbm.at[0, :, block(1 - g, half)], WD.at[block(g, hid)], dss, drs)
    wg_copy.start()
    wu_copy.start()
    wd_copy.start()
    wd_across.start()

    def second_axis(i, h):
        in_half(
            h,
            [lambda: landed(B.at[i, h, 0:32], rs.at[A_AG, i, h])],
            [lambda: landed(B.at[i, h, 0:64], rs.at[A_AG, i, h])],
        )
        for k in (1, 3):
            b_ag(i, h, k).start()

    def pass_on(i, h):
        landed(B.at[i, h, 0:128], rs.at[B_AG, i, h])
        for k in (1, 3):
            b_on(i, h, k).start()

    for r in range(3):
        landed(IB.at[r, 0, 0:3], irs.at[0, r])
        for k in (1, 2, 3):
            info_b(r, k).start()

    stages((of(second_axis, 0), 0))
    stages((of(second_axis, 1), 0), (of(pass_on, 0), 0))

    acc[...] = jnp.zeros_like(acc)

    lane = lax.broadcasted_iota(jnp.int32, (8, 128), 1)
    seg_mask = [(lane >= 32 * a) & (lane < 32 * a + 32) for a in range(4)]
    lane1 = lax.broadcasted_iota(jnp.int32, (16, 128), 1)
    seg16 = sum(jnp.where(lane1 >= 32 * a, 1, 0) for a in (1, 2, 3))
    row1 = lax.broadcasted_iota(jnp.int32, (16, 128), 0)
    odd = jnp.where(((row1 >= 4) & (row1 < 8)) | (row1 >= 12), 1, 0)
    src8 = (odd * 4 + seg16).astype(F32)
    ti = lax.broadcasted_iota(jnp.int32, (128, 128), 0)
    tj = lax.broadcasted_iota(jnp.int32, (128, 128), 1)
    start_j = sum(jnp.where(tj >= 32 * a, 32, 0) for a in (1, 2, 3))
    before = jnp.where((ti < tj) & (ti >= start_j), 1.0, 0.0).astype(BF)
    iota_q = lax.broadcasted_iota(jnp.int32, (80, 128), 0).astype(F32)
    iota_k = lax.broadcasted_iota(jnp.int32, (128, 320), 1).astype(F32)

    for r in range(3):
        a_ax, b_ax, c_ax = axes(r, g)
        landed(IB.at[r, 0:3], irs.at[1, r])
        hits, weights = [], []
        for pair in range(4):
            h, first = pair // 2, pair % 2 * 2
            from_a = [
                2 * (s % 2) + lax.rem(h + first + s // 2 + coord(c_ax), 2) for s in range(4)
            ]
            dest = sum(jnp.where(seg_mask[s], IB[r, first + s // 2, from_a[s], 0:8, :], 0.0) for s in range(4))
            wts = sum(jnp.where(seg_mask[s], IB[r, first + s // 2, from_a[s], 8:16, :], 0.0) for s in range(4))
            for d in range(4):
                target = (dev + (d - coord(c_ax)) * stride(c_ax)).astype(F32)
                hit = dest == target
                hits.append(jnp.sum(jnp.where(hit, 1.0, 0.0), axis=0, keepdims=True))
                weights.append(jnp.sum(jnp.where(hit, wts, 0.0), axis=0, keepdims=True))
        hits = jnp.concatenate(hits, axis=0)
        weights = jnp.concatenate(weights, axis=0)
        rank = dot(hits.astype(BF), before)
        at_row = jnp.where(rank < MAIN, src8 * MAIN + rank, 64 + src8 * REST + (rank - MAIN))
        at_row = jnp.where(hits > 0, at_row, -1000.0)
        fill = jnp.zeros((112, 128), F32)
        place_t = jnp.transpose(jnp.concatenate([at_row, fill], axis=0))
        weights_t = jnp.transpose(jnp.concatenate([weights, fill], axis=0))
        for pair in range(4):
            total = jnp.zeros((128, 320), F32)
            cols = slice(pair % 2 * 128, pair % 2 * 128 + 128)
            for d in range(4):
                at = pair * 4 + d
                SEL[r, pair // 2, d * 80 : d * 80 + 80, cols] = jnp.where(
                    iota_q == at_row[at : at + 1, :], 1.0, 0.0
                ).astype(BF)
                total = total + jnp.where(
                    iota_k == place_t[:, at : at + 1] + 80.0 * d, weights_t[:, at : at + 1], 0.0
                )
            WT[r, pair // 2, cols, :] = total.astype(BF)

    def select(i, h):
        r = lax.rem(i, 3)
        a, b, c = axes(r, g)
        landed(B.at[i, h, 0:64], rs.at[B_ON, i, h])
        SB[i, h] = dot(SEL[r, h], B[i, h]).astype(BF).reshape(4, 80, CW)
        for k in (1, 2, 3):
            c_out(i, h, k).start()
        X[i, h, coord(c)] = SB[i, h, coord(c)]

    def multiply(rows_ref, i, h, core):
        rho, _, _ = axes(lax.rem(i, 3), core)
        rows = rows_ref[i, h].reshape(320, CW)
        depth = pl.ds(pl.multiple_of(core * half + i * CW, CW), CW)
        for w, weight in enumerate((WG, WU)):
            acc[w, rho, h * 320 : h * 320 + 320, :] += dot(rows, weight[depth, :])

    def arrived(i, h):
        rho, _, _ = axes(lax.rem(i, 3), g)
        landed(X.at[i, h, 0:3], rs.at[C_OUT, i, h])
        rest = jnp.concatenate([X[i, h, c, 64:80, :] for c in range(4)], axis=0)
        rest = dot(perm[0, rho, h], rest).astype(BF)
        for c in range(4):
            X[i, h, c, 64:80, :] = rest[c * 16 : c * 16 + 16, :]
        rows_across(i, h).start()
        multiply(X, i, h, g)

    def crossed(i, h):
        rows_across(i, h).wait_recv()
        multiply(XP, i, h, 1 - g)

    def swiglu(gate, up):
        return gate / (1.0 + jnp.exp(-gate)) * up

    def hidden(h):
        own = [q for q in np.ndindex(4, 4, 4) if sum(q) % 2 == h]
        for q in own:
            rows = [slice(main_row(q, rho), main_row(q, rho) + MAIN) for rho in range(3)]
            gate = acc[0, 0, rows[0], :] + acc[0, 1, rows[1], :] + acc[0, 2, rows[2], :]
            up = acc[1, 0, rows[0], :] + acc[1, 1, rows[1], :] + acc[1, 2, rows[2], :]
            acc[0, 0, rows[0], :] = swiglu(gate, up)
        rest_at = [(h * 4 + c) * 80 + 64 for c in range(4)]
        for at in rest_at:
            rows = slice(at, at + 16)
            gate = acc[0, 0, rows, :] + acc[0, 1, rows, :] + acc[0, 2, rows, :]
            up = acc[1, 0, rows, :] + acc[1, 1, rows, :] + acc[1, 2, rows, :]
            acc[0, 0, rows, :] = swiglu(gate, up)

        rest = jnp.concatenate([acc[0, 0, at : at + 16, :] for at in rest_at], axis=0).astype(BF)
        for rho in range(3):
            for q in own:
                if q[rho] >= 2:
                    continue
                two = list(q)
                two[rho] += 2
                here = main_row(q, rho)
                one, other = main_row(q, 0), main_row(two, 0)
                HR[rho, g, here : here + 16, :] = jnp.concatenate(
                    [acc[0, 0, one : one + MAIN, :], acc[0, 0, other : other + MAIN, :]], axis=0
                ).astype(BF)
            turned = dot(perm[1, rho, h], rest).astype(BF)
            for c in range(4):
                HR[rho, g, rest_at[c] : rest_at[c] + 16, :] = turned[c * 16 : c * 16 + 16, :]
        for r in range(3):
            hidden_across(lax.rem(r + 1 - g, 3), h).start()

    def down(i, h):
        rho, _, c = axes(lax.rem(i, 3), g)

        @pl.when(i < 3)
        def _():
            hidden_across(rho, h).wait_recv()

        rows = slice(h * 320, h * 320 + 320)
        cols = block(i, CW)
        both = jnp.concatenate([HR[rho, 0, rows, :], HR[rho, 1, rows, :]], axis=1)
        SB[i, h] = dot(both, WD[:, cols]).astype(BF).reshape(4, 80, CW)
        for k in (1, 2, 3):
            c_back(i, h, k).start()
        RB[i, h, coord(c)] = SB[i, h, coord(c)]

    def combine(i, h):
        r = lax.rem(i, 3)
        landed(RB.at[i, h, 0:3], rs.at[C_BACK, i, h])
        rows = RB[i, h].reshape(320, CW)
        B[i, h] = dot(WT[r, h], rows).astype(BF)
        for k in (1, 2, 3):
            b_rs(i, h, k).start()

    def first_axis(i, h):
        a, b, c = axes(lax.rem(i, 3), g)
        landed(RSB.at[i, h], rs.at[B_RS, i, h])
        total = B[i, h, block(coord(b), 64), :].astype(F32)
        for k in range(3):
            total = total + RSB[i, h, k].astype(F32)
        QB[i, h] = total.astype(BF)
        in_half(h, [lambda: a_rs(i, 2).start()], [lambda: a_rs(i, 1).start(), lambda: a_rs(i, 3).start()])

    def finish(i):
        a, b, c = axes(lax.rem(i, 3), g)
        landed(RA.at[i], rs.at[A_RS, i, 0])
        total = QB[i, parity, block(lax.div(coord(a), 2), 32), :].astype(F32)
        for k in range(3):
            total = total + RA[i, k].astype(F32)
        out[:, block(i, CW)] = total.astype(BF)

    stages((of(pass_on, 1), 0))
    stages((of(select, 0), 0))
    stages((of(select, 1), 0))
    wg_copy.wait()
    wu_copy.wait()
    stages((of(arrived, 0), 0), (of(crossed, 0), 1))
    hidden(0)
    wd_copy.wait()
    wd_across.wait()
    loop(0, EARLY, of(arrived, 1))
    sent(X.at[:, 0, 0:3], ss.at[C_OUT, 0])
    stages((of(down, 0), 0))
    for h in range(2):
        sent(B.at[:, h, 0:128], ss.at[B_AG, h])
        sent(B.at[:, h, 0:64], ss.at[B_ON, h])
    stages((of(arrived, 1), 0, EARLY, n), (of(crossed, 1), 1), (of(combine, 0), COMBINE, 0, SPLIT))
    hidden(1)
    loop(SPLIT, n, of(combine, 0))
    sent(X.at[:, 1, 0:3], ss.at[C_OUT, 1])
    stages((of(down, 1), 0), (of(first_axis, 0), FIRST), (of(combine, 1), PACE[0]), (of(first_axis, 1), PACE[1]), (finish, PACE[2]))

    sent(B.at[:, 0, 0:96], ss.at[A_AG, 0])
    for h in range(2):
        sent(RB.at[:, h, 0:3], ss.at[C_BACK, h])
        sent(RSB.at[:, h], ss.at[B_RS, h])
    sent(RA, ss.at[A_RS, 0])
    sent(XP, ess)
    sent(HR.at[:, 0], hss)
    sent(IB.at[:, 0, 0:3], iss.at[0])
    sent(IB.at[:, 0:3], iss.at[1])


def body(tokens, routes, route_weights, placement, w_gate, w_up, w_down):
    local_tokens, half = tokens.shape
    n = half // CW
    hid = w_gate.shape[2]
    perm = jnp.asarray(rest_matrices(), BF)
    vmem = pl.BlockSpec(memory_space=pltpu.VMEM)
    hbm = pl.BlockSpec(memory_space=pl.ANY)
    dma = pltpu.SemaphoreType.DMA
    return pl.pallas_call(
        kernel,
        out_shape=jax.ShapeDtypeStruct(tokens.shape, BF),
        in_specs=[vmem, vmem, vmem, pl.BlockSpec(memory_space=pltpu.SMEM), vmem, hbm, hbm, hbm],
        out_specs=vmem,
        scratch_shapes=[
            pltpu.VMEM((2 * half, hid), BF),
            pltpu.VMEM((2 * half, hid), BF),
            pltpu.VMEM((2 * hid, half), BF),
            pltpu.VMEM((n, 2, 256, CW), BF),
            pltpu.VMEM((n, 2, 4, 80, CW), BF),
            pltpu.VMEM((n, 2, 4, 80, CW), BF),
            pltpu.VMEM((n, 2, 4, 80, CW), BF),
            pltpu.VMEM((2, 3, 640, hid), F32),
            pltpu.VMEM((3, 2, 640, hid), BF),
            pltpu.VMEM((n, 2, 4, 80, CW), BF),
            pltpu.VMEM((n, 2, 3, 64, CW), BF),
            pltpu.VMEM((n, 3, 32, CW), BF),
            pltpu.VMEM((n, 2, 64, CW), BF),
            pltpu.VMEM((3, 4, 4, 16, 128), F32),
            pltpu.VMEM((3, 2, 320, 256), BF),
            pltpu.VMEM((3, 2, 256, 320), BF),
            pltpu.VMEM((16, 128), F32),
            dma((7, 2)),
            dma((7, n, 2)),
            dma((2,)),
            dma((2, 3)),
            dma,
            dma((n, 2)),
            dma,
            dma((3, 2)),
            dma((3,)),
            dma,
            dma,
        ],
        compiler_params=pltpu.CompilerParams(
            collective_id=0, has_side_effects=True, vmem_limit_bytes=64 * 1024 * 1024 - 512 * 1024
        ),
    )(tokens, routes.T, route_weights.T, placement, perm, w_gate, w_up, w_down)


def solution(mesh):
    in_specs = (
        P("dev", "group"),
        P("dev", None),
        P("dev", None),
        P(),
        P("dev", None, "group"),
        P("dev", None, "group"),
        P("dev", "group", None),
    )
    out_specs = P("dev", "group")
    return jax.shard_map(body, mesh=mesh, in_specs=in_specs, out_specs=out_specs, check_vma=False)
```
